512 devices in a mesh: row: 16 (over z_lo, x), col: 32 (over z_hi, y, core).
Axes of the slice: x: 4, y: 4, z: 16 (z_hi: 4, z_lo: 4; z = z_hi * 4 + z_lo), core: 2. Of those that a mesh axis runs over, the one named last changes fastest.
Arguments:
- b_diag: float32 [512, 512], P('row'), as said below
- a_diag: float32 [512, 512], P('row'), as said below
- b_panel: float32 [16384, 512], P(('row', 'col')), may hold values from -2 to 2
- a_panel: float32 [16384, 512], P(('row', 'col')), may hold values from -2 to 2
- a_trail: float32 [16384, 16384], P('row', 'col'), as said below
Outputs:
- a_diag_new: float32 [512, 512], P('row')
- l_panel: float32 [16384, 512], P(('row', 'col'))
- a_panel_new: float32 [16384, 512], P(('row', 'col'))
- a_trail_new: float32 [16384, 16384], P('row', 'col')
The draws below stay inside these ranges and needn't reach their ends.
Inputs may be any that keep to these rules, and one draw needn't show every extreme that they name: b_diag is symmetric positive definite, its smallest eigenvalue 0.5 or more. a_diag is symmetric. a_trail is symmetric.
All inputs are finite; a program needn't handle non-finite values.
Results may differ from the reference program's by a relative error of at most 0.0001.
Values sent between devices are 32-bit elements; how exact they have to be, the bound alone decides.
A program may use at most 64 MiB of HBM per device.

```python
import jax
import jax.numpy as jnp
from jax import lax

NB = 512
ORDER = 16384


def draw_b_diag(key, part):
    first = jax.random.fold_in(key, 11)
    second = jax.random.fold_in(key, 12)
    factor_rows = jax.random.normal(first, (NB, NB), jnp.float32) * (0.7 / NB ** 0.5)
    shifts = jax.random.uniform(second, (NB,), jnp.float32, 0.5, 1.5)
    product = jnp.dot(factor_rows, factor_rows.T, precision=lax.Precision.HIGHEST)
    return 0.5 * (product + product.T) + jnp.diag(shifts)


def draw_a_diag(key, part):
    values = jax.random.normal(jax.random.fold_in(key, 21), (NB, NB), jnp.float32)
    return (values + values.T) * (0.05 / 2.0 ** 0.5)


def draw_a_trail(key, part):
    values = jax.random.normal(jax.random.fold_in(key, 31), (ORDER, ORDER), jnp.float32)
    return (values + values.T) * (0.5 / 2.0 ** 0.5)


def level_of(key, dims, cuts, low, high):
    level = 1.0
    for axis_at, parts in cuts:
        heights = jax.random.uniform(jax.random.fold_in(jax.random.fold_in(key, 6), axis_at), (parts,), jnp.float32, low / len(cuts), high / len(cuts))
        level = level * jnp.repeat(jnp.exp(heights), dims[axis_at] // parts).reshape((-1,) + (1,) * (len(dims) - 1 - axis_at))
    return level


def scatter_about(own_key, shape, deviation, limit, cuts=(), kind=jnp.bfloat16):
    result = jax.random.normal(own_key, shape, jnp.float32) * deviation
    if len(cuts) > 0:
        result = level_of(own_key, shape, cuts, -0.22, 0.18) * result
    return jnp.clip(result, min=-limit, max=limit).astype(kind)


def setup_inputs(seed: int = 0) -> dict:
    streams_of = jax.random.split(jax.random.key(seed), 6)
    b_diag = draw_b_diag(jax.random.fold_in(streams_of[5], 71), 0)
    a_diag = draw_a_diag(jax.random.fold_in(streams_of[5], 71), 0)
    b_panel = scatter_about(streams_of[2], (ORDER, NB), 0.3, 2.0, ((0, 512),), jnp.float32)
    a_panel = scatter_about(streams_of[3], (ORDER, NB), 0.3, 2.0, ((0, 512),), jnp.float32)
    a_trail = draw_a_trail(jax.random.fold_in(streams_of[5], 71), 0)
    return dict(b_diag=b_diag, a_diag=a_diag, b_panel=b_panel, a_panel=a_panel, a_trail=a_trail)


HIGHEST = lax.Precision.HIGHEST

def matmul(left, right):
    return jnp.dot(left.astype(jnp.float32), right.astype(jnp.float32), precision=HIGHEST, preferred_element_type=jnp.float32)

def reference(b_diag, a_diag, b_panel, a_panel, a_trail):
    factor = jnp.linalg.cholesky(b_diag)
    identity = jnp.eye(b_diag.shape[0], dtype=b_diag.dtype)
    inverse = jax.scipy.linalg.solve_triangular(factor, identity, lower=True)
    a_diag_new = matmul(matmul(inverse, a_diag), inverse.T)
    l_panel = matmul(b_panel, inverse.T)
    correction = 0.5 * matmul(l_panel, a_diag_new)
    mixed = matmul(a_panel, inverse.T) - correction
    a_trail_new = a_trail - matmul(mixed, l_panel.T) - matmul(l_panel, mixed.T)
    a_panel_new = mixed - correction
    return (a_diag_new, l_panel, a_panel_new, a_trail_new)
```

```python
import functools

import jax
import jax.numpy as jnp
from jax import lax
from jax.experimental import pallas as pl
from jax.experimental.pallas import tpu as pltpu
from jax.sharding import Mesh
from jax.sharding import PartitionSpec as P

f32 = jnp.float32
bf16 = jnp.bfloat16
MESH = pl.DeviceIdType.MESH
HIGHEST = lax.Precision.HIGHEST
NN = ((1,), (0,))
NT = ((1,), (1,))


def dot(a, b, dims):
    return lax.dot_general(a, b, (dims, ((), ())), precision=HIGHEST, preferred_element_type=f32)


def halves(x):
    hi = x.astype(bf16)
    return hi, (x - hi.astype(f32)).astype(bf16)


def dot3(a, b, dims):
    def one(u, v):
        return lax.dot_general(u, v, (dims, ((), ())), preferred_element_type=f32)

    return one(a[0], b[0]) + (one(a[0], b[1]) + one(a[1], b[0]))


def lane_bcast(x, j):
    return jnp.broadcast_to(x[:, j : j + 1], (8, 128))


def sub_bcast(x, k):
    return jnp.broadcast_to(x[k : k + 1, :], (8, 128))


def base64(block, odd):
    lane = lax.broadcasted_iota(jnp.int32, (8, 128), 1)
    sub = lax.broadcasted_iota(jnp.int32, (8, 128), 0)
    to, at = 64 * odd, 64 - 64 * odd
    mine = (lane >= 64) if odd else (lane < 64)
    turned = pltpu.roll(block, 64, 1)
    rows_of = []
    for g in range(8):
        eye = jnp.where(lane == sub + (8 * g + to), 1.0, 0.0).astype(f32)
        rows_of.append(jnp.where(mine, eye, turned[8 * g : 8 * g + 8, :]))
    out = []
    for g in range(8):
        rows = rows_of[g]
        cols = [lane_bcast(rows, at + 8 * g + k) for k in range(8)]
        done = jnp.zeros((8, 128), f32)
        for k in range(8):
            is_k = sub == k
            row = sub_bcast(rows, k)
            pivot = sub_bcast(cols[k], k)
            inv = 1.0 / pivot
            done = jnp.where(is_k, row * lax.rsqrt(pivot), done)
            m = cols[k] * inv
            rows = jnp.where(is_k, row * inv, rows - m * row)
            for j in range(k + 1, 8):
                top = sub_bcast(cols[j], k)
                cols[j] = jnp.where(is_k, top * inv, cols[j] - m * top)
        out.append(jnp.where(mine, done, 0.0))
        if g < 7:
            tops = [sub_bcast(rows, k) for k in range(8)]
            for i in range(g + 1, 8):
                t = [lane_bcast(rows_of[i], at + 8 * g + k) * tops[k] for k in range(8)]
                rows_of[i] = rows_of[i] - (((t[0] + t[1]) + (t[2] + t[3])) + ((t[4] + t[5]) + (t[6] + t[7])))
    return jnp.concatenate(out, axis=0)


def invert(aw, between):
    following = None
    for k in range(8):
        odd = k % 2
        w0, r0 = 64 * (k - odd), 64 * k
        own = base64(aw[r0 : r0 + 64, w0 : w0 + 128], odd) if k == 0 else following
        c0 = 64 * (k + 1) if odd else 64 * k
        c1 = 512 + 64 * (k + 1) if odd else 512 + 64 * (k + 2)
        if k < 7:
            odd_next = (k + 1) % 2
            n0 = 64 * (k + 1 - odd_next)
            left = dot(aw[r0 + 64 : r0 + 128, w0 : w0 + 128], own, NT)
            right = dot(own, aw[w0 : w0 + 128, n0 : n0 + 128], NN)
            following = base64(aw[r0 + 64 : r0 + 128, n0 : n0 + 128] - dot(left, right, NN), odd_next)
        right = dot(own, aw[w0 : w0 + 128, c0:c1], NN)
        if k < 7:
            left = dot(aw[r0 + 64 : 512, w0 : w0 + 128], own, NT)
            aw[r0 + 64 : 512, c0:c1] = aw[r0 + 64 : 512, c0:c1] - dot(left, right, NN)
        aw[r0 : r0 + 64, 512:c1] = right[:, 512 - c0 :]
        between(k)


class Copies:
    def __init__(self, send, recv):
        self.send, self.recv, self.sent = send, recv, []

    def describe(self, n, src, dst, dev):
        return pltpu.make_async_remote_copy(
            src_ref=src, dst_ref=dst, send_sem=self.send.at[n], recv_sem=self.recv.at[n], device_id=dev, device_id_type=MESH
        )

    def start(self, n, src, dst, dev):
        copy = self.describe(n, src, dst, dev)
        copy.start()
        self.sent.append(copy)

    def arrived(self, n, dst, dev):
        self.describe(n, dst, dst, dev).wait_recv()

    def finish(self):
        for copy in self.sent:
            copy.wait_send()


def kernel(
    b_diag, a_diag, b_panel, a_panel, a_trail,
    diag_out, l_out, n_out, trail_out,
    aw, bd, ad, pr, pc, st, adn, mid, trail, zh, zl,
    send, recv, local, tin, tout,
):
    zlo, x, zhi, y, core = (lax.axis_index(a) for a in ("z_lo", "x", "z_hi", "y", "core"))
    grid_row = zlo * 4 + x
    other = 1 - core

    def up(i, d):
        return lax.rem(i + d, 4)

    load_trail = pltpu.make_async_copy(a_trail, trail, tin.at[0])

    def place(zh_, y_, c_):
        return pl.ds(pl.multiple_of((zh_ * 8 + y_ * 2 + c_) * 32, 32), 32)

    own = place(zhi, y, core)
    own_b = pltpu.make_async_copy(b_panel, pr.at[own, pl.ds(0, 512)], local.at[0])
    own_a = pltpu.make_async_copy(a_panel, pr.at[own, pl.ds(512, 512)], local.at[1])
    half = pl.ds(pl.multiple_of(core * 16, 16), 16)
    own_bd = pltpu.make_async_copy(b_diag.at[half], bd.at[zlo, x, core], local.at[2])
    own_ad = pltpu.make_async_copy(a_diag.at[half], ad.at[zlo, x, core], local.at[3])
    own_bd.start()
    own_b.start()
    own_a.start()
    own_ad.start()

    peers = []
    peers += [{"z_lo": up(zlo, d)} for d in (1, 2, 3)]
    peers += [{"x": up(x, d), "core": c} for d in (1, 3) for c in (0, 1)]
    peers += [{"z_hi": up(zhi, d)} for d in (1, 3)]
    peers += [{"y": up(y, d)} for d in (1, 3)]
    peers += [{"core": other}]
    turned = {"z_lo": zhi, "x": y, "z_hi": zlo, "y": x}
    stays = jnp.logical_and(zlo == zhi, x == y)
    barrier = pltpu.get_barrier_semaphore()
    for dev in peers:
        pl.semaphore_signal(barrier, inc=1, device_id=dev, device_id_type=MESH)

    @pl.when(jnp.logical_not(stays))
    def _():
        pl.semaphore_signal(barrier, inc=1, device_id=turned, device_id_type=MESH)

    pl.semaphore_wait(barrier, len(peers) + 1 - stays.astype(jnp.int32))

    copies = Copies(send, recv)
    X = {1: {"x": up(x, 1)}, -1: {"x": up(x, 3)}}
    Y = {1: {"y": up(y, 1)}, -1: {"y": up(y, 3)}}
    Z = {1: {"z_hi": up(zhi, 1)}, -1: {"z_hi": up(zhi, 3)}}
    CORE = {"core": other}

    def diag_z(base, buf):
        for d in (1, 2, 3):
            copies.start(base + d - 1, buf.at[zlo, x, core], buf.at[zlo, x, core], {"z_lo": up(zlo, d)})

    def diag_x(base, buf):
        for d in (1, 2, 3):
            copies.arrived(base + d - 1, buf.at[up(zlo, 4 - d), x, core], {"z_lo": up(zlo, d)})
        mine = buf.at[:, x, core]
        copies.start(base + 3, mine, mine, X[1])
        copies.start(base + 4, mine, mine, X[-1])
        copies.start(base + 5, mine, mine, CORE)

    def diag_forward(base, buf):
        left, right = up(x, 3), up(x, 1)
        copies.arrived(base + 3, buf.at[:, left, core], X[1])
        part = buf.at[pl.ds(0, 2), left, core]
        copies.start(base + 6, part, part, X[1])
        copies.start(base + 8, buf.at[:, left, core], buf.at[:, left, core], CORE)
        copies.arrived(base + 4, buf.at[:, right, core], X[-1])
        part = buf.at[pl.ds(2, 2), right, core]
        copies.start(base + 7, part, part, X[-1])
        copies.start(base + 9, buf.at[:, right, core], buf.at[:, right, core], CORE)

    def diag_last(base, buf):
        far = up(x, 2)
        copies.arrived(base + 6, buf.at[pl.ds(0, 2), far, core], X[1])
        copies.arrived(base + 7, buf.at[pl.ds(2, 2), far, core], X[-1])
        copies.start(base + 10, buf.at[:, far, core], buf.at[:, far, core], CORE)

    def diag_end(base, buf):
        for n, place_x in ((5, x), (8, up(x, 3)), (9, up(x, 1)), (10, up(x, 2))):
            copies.arrived(base + n, buf.at[:, place_x, other], CORE)

    BD, AD = 0, 11

    ROWZ, ROWY, ROWC = 22, 26, 38
    offsets = (0, 3, 1, 2)

    def piece(o, dy, c):
        return pr.at[place(up(zhi, offsets[o]), up(y, dy), c)]

    def part_of(o, dy, c, h):
        start = (up(zhi, offsets[o]) * 8 + up(y, dy) * 2 + c) * 32 + 16 * h
        return pr.at[pl.ds(pl.multiple_of(start, 16), 16)]

    def rows_z():
        copies.start(ROWZ, piece(0, 0, core), piece(0, 0, core), Z[1])
        copies.start(ROWZ + 1, piece(0, 0, core), piece(0, 0, core), Z[-1])

    def rows_z_forward():
        copies.arrived(ROWZ, piece(1, 0, core), Z[1])
        copies.start(ROWZ + 2, part_of(1, 0, core, 0), part_of(1, 0, core, 0), Z[1])
        copies.arrived(ROWZ + 1, piece(2, 0, core), Z[-1])
        copies.start(ROWZ + 3, part_of(2, 0, core, 1), part_of(2, 0, core, 1), Z[-1])

    def rows_z_last():
        copies.arrived(ROWZ + 2, part_of(3, 0, core, 0), Z[1])
        copies.arrived(ROWZ + 3, part_of(3, 0, core, 1), Z[-1])

    def rows_y(o):
        p = piece(o, 0, core)
        copies.start(ROWY + 3 * o, p, p, Y[1])
        copies.start(ROWY + 3 * o + 1, p, p, Y[-1])
        copies.start(ROWC + 4 * o, p, p, CORE)

    def rows_y_forward(o):
        copies.arrived(ROWY + 3 * o, piece(o, 3, core), Y[1])
        if o < 2:
            copies.start(ROWY + 3 * o + 2, piece(o, 3, core), piece(o, 3, core), Y[1])
        copies.arrived(ROWY + 3 * o + 1, piece(o, 1, core), Y[-1])
        if o >= 2:
            copies.start(ROWY + 3 * o + 2, piece(o, 1, core), piece(o, 1, core), Y[-1])
        copies.start(ROWC + 4 * o + 1, piece(o, 3, core), piece(o, 3, core), CORE)
        copies.start(ROWC + 4 * o + 2, piece(o, 1, core), piece(o, 1, core), CORE)

    def rows_y_last(o):
        copies.arrived(ROWY + 3 * o + 2, piece(o, 2, core), Y[1] if o < 2 else Y[-1])
        copies.start(ROWC + 4 * o + 3, piece(o, 2, core), piece(o, 2, core), CORE)

    def rows_end():
        for o in range(4):
            for n, dy in ((0, 0), (1, 3), (2, 1), (3, 2)):
                copies.arrived(ROWC + 4 * o + n, piece(o, dy, other), CORE)

    TURN, COLZ, COLX = 54, 55, 58

    def turn():
        @pl.when(stays)
        def _():
            pltpu.make_async_copy(pr.at[own], st.at[zhi], recv.at[TURN]).start()

        @pl.when(jnp.logical_not(stays))
        def _():
            copies.describe(TURN, pr.at[own], st.at[zhi], turned).start()

    def turned_here():
        @pl.when(stays)
        def _():
            pltpu.make_async_copy(pr.at[own], st.at[zhi], recv.at[TURN]).wait()

        @pl.when(jnp.logical_not(stays))
        def _():
            copies.arrived(TURN, st.at[zlo], turned)

    def turn_sent():
        @pl.when(jnp.logical_not(stays))
        def _():
            copies.describe(TURN, pr.at[own], st.at[zhi], turned).wait_send()

    def cols_z():
        for d in (1, 2, 3):
            copies.start(COLZ + d - 1, st.at[zlo], st.at[zlo], {"z_lo": up(zlo, d)})

    def cols_z_end():
        for d in (1, 2, 3):
            copies.arrived(COLZ + d - 1, st.at[up(zlo, 4 - d)], {"z_lo": up(zlo, d)})

    def spot(i, v, s):
        return pc.at[pl.ds(pl.multiple_of((i * 8 + v * 2 + s) * 32, 32), 32)]

    def col_copy(way, h, s, dev):
        n = COLX + 4 * way + 2 * (h % 2)
        return pltpu.make_async_remote_copy(
            src_ref=st.at[h], dst_ref=spot(h % 2, x, s), send_sem=send.at[COLX + 4 * way + h],
            recv_sem=recv.at[n + s], device_id=dev, device_id_type=MESH,
        )

    def on_core(s, h, there):
        n = COLX + 8 + 2 * (h % 2) + s
        if h // 2 == s:
            return pltpu.make_async_copy(st.at[h], spot(h % 2, x, s), recv.at[n])
        return col_copy(2, h, s, {"core": 1 - s})

    def cols_x():
        for s in (0, 1):

            @pl.when(core == s)
            def _(s=s):
                for h in range(4):
                    for way, dx in ((0, 1), (1, 3)):
                        col_copy(way, h, s, {"x": up(x, dx), "core": h // 2}).start()
                    on_core(s, h, None).start()

    def cols_x_sent():
        for s in (0, 1):

            @pl.when(core == s)
            def _(s=s):
                for h in range(4):
                    for way, dx in ((0, 1), (1, 3)):
                        col_copy(way, h, s, {"x": up(x, dx), "core": h // 2}).wait_send()
                    if h // 2 != s:
                        on_core(s, h, None).wait_send()

    FAR = COLX + 16

    def cols_forward():
        for i in (0, 1):
            for s in (0, 1):
                copies.arrived(COLX + 2 * i + s, spot(i, up(x, 3), s), X[1])
                copies.arrived(COLX + 4 + 2 * i + s, spot(i, up(x, 1), s), X[-1])
            p = spot(i, up(x, 3), 0)
            copies.start(FAR + 2 * i, p, p, X[1])
            p = spot(i, up(x, 1), 1)
            copies.start(FAR + 2 * i + 1, p, p, X[-1])

    def cols_end():
        for i in (0, 1):
            for s in (0, 1):
                copies.arrived(COLX + 8 + 2 * i + s, spot(i, x, s), CORE)
                copies.arrived(FAR + 2 * i + s, spot(i, up(x, 2), s), X[1])

    own_bd.wait()
    diag_z(BD, bd)
    own_b.wait()
    own_a.wait()
    rows_z()
    turn()
    rows_y(0)
    load_trail.start()
    diag_x(BD, bd)
    own_ad.wait()
    diag_z(AD, ad)
    diag_forward(BD, bd)
    diag_last(BD, bd)
    eye = lax.broadcasted_iota(jnp.int32, (512, 512), 0) == lax.broadcasted_iota(jnp.int32, (512, 512), 1)
    aw[:, 512:] = jnp.where(eye, 1.0, 0.0).astype(f32)
    diag_end(BD, bd)
    aw[:, :512] = bd[...].reshape(512, 512)

    def between(k):
        if k == 0:
            turned_here()
            cols_z()
            rows_y_forward(0)
            diag_x(AD, ad)
        if k == 1:
            rows_z_forward()
            rows_y(1)
            rows_y(2)
        if k == 2:
            cols_z_end()
            cols_x()
            rows_y_last(0)
            diag_forward(AD, ad)
        if k == 3:
            rows_y_forward(1)
            rows_y_forward(2)
            diag_last(AD, ad)
        if k == 4:
            rows_z_last()
            rows_y(3)
        if k == 5:
            rows_y_last(1)
            rows_y_last(2)
        if k == 6:
            rows_y_forward(3)
        if k == 7:
            cols_forward()

    invert(aw, between)
    diag_end(AD, ad)
    mid[...] = dot(ad[...].reshape(512, 512), aw[:, 512:], NT)
    rows_y_last(3)
    w = halves(aw[:, 512:])
    adn[...] = dot(aw[:, 512:], mid[...], NN)
    diag_out[...] = adn[pl.ds(pl.multiple_of(grid_row * 32, 32), 32), :]
    q = halves(adn[...])
    own_l = dot3(halves(pr[own, 0:512]), w, NT)
    l_out[...] = own_l
    n_out[...] = dot3(halves(pr[own, 512:1024]), w, NT) - dot3(halves(own_l), q, NN)
    cols_end()
    col_l = dot3(halves(pc[:, 0:512]), w, NT)
    lh = halves(col_l)
    col_n = dot3(halves(pc[:, 512:1024]), w, NT) - dot3(lh, q, NN)
    col_y = dot3(lh, w, NN)
    col_z = dot3(halves(col_n), w, NN)
    zh[:, 0:512], zl[:, 0:512] = halves(col_z)
    zh[:, 512:1024], zl[:, 512:1024] = halves(col_y)
    load_trail.wait()
    rows_end()

    def store(t):
        tile = pl.ds(pl.multiple_of(t * 128, 128), 128)
        return pltpu.make_async_copy(trail.at[tile], trail_out.at[tile], tout.at[t])

    @pl.loop(0, 8)
    def _(t):
        tile = pl.ds(pl.multiple_of(t * 128, 128), 128)
        trail[tile, :] = trail[tile, :] - dot3(halves(pr[tile, :]), (zh[...], zl[...]), NT)
        store(t).start()

    copies.finish()
    turn_sent()
    cols_x_sent()
    for t in range(8):
        store(t).wait()


def shards(*arrays):
    vmem = pl.BlockSpec(memory_space=pltpu.VMEM)
    anywhere = pl.BlockSpec(memory_space=pl.ANY)
    own = jax.ShapeDtypeStruct((32, 512), f32)
    return pl.pallas_call(
        kernel,
        out_shape=(own, own, own, jax.ShapeDtypeStruct((1024, 512), f32)),
        in_specs=[anywhere] * 5,
        out_specs=(vmem, vmem, vmem, anywhere),
        scratch_shapes=[
            pltpu.VMEM((512, 1024), f32),
            pltpu.VMEM((4, 4, 2, 16, 512), f32),
            pltpu.VMEM((4, 4, 2, 16, 512), f32),
            pltpu.VMEM((1024, 1024), f32),
            pltpu.VMEM((512, 1024), f32),
            pltpu.VMEM((4, 32, 1024), f32),
            pltpu.VMEM((512, 512), f32),
            pltpu.VMEM((512, 512), f32),
            pltpu.VMEM((1024, 512), f32),
            pltpu.VMEM((512, 1024), bf16),
            pltpu.VMEM((512, 1024), bf16),
            pltpu.SemaphoreType.DMA((80,)),
            pltpu.SemaphoreType.DMA((80,)),
            pltpu.SemaphoreType.DMA((4,)),
            pltpu.SemaphoreType.DMA((1,)),
            pltpu.SemaphoreType.DMA((8,)),
        ],
        compiler_params=pltpu.CompilerParams(collective_id=0, has_side_effects=True, vmem_limit_bytes=56 << 20),
        cost_estimate=pl.CostEstimate(flops=10**10, bytes_accessed=8 << 20, transcendentals=0),
    )(*arrays)


def solution(mesh):
    names = ("z_lo", "x", "z_hi", "y", "core")
    split = Mesh(mesh.devices.reshape(4, 4, 4, 4, 2), names)
    row, col = names[:2], names[2:]
    return jax.shard_map(
        shards,
        mesh=split,
        in_specs=(P(row, None), P(row, None), P(names, None), P(names, None), P(row, col)),
        out_specs=(P(row, None), P(names, None), P(names, None), P(row, col)),
        check_vma=False,
    )
```

```python
import functools

import jax
import jax.numpy as jnp
from jax import lax
from jax.experimental import pallas as pl
from jax.experimental.pallas import tpu as pltpu
from jax.sharding import Mesh
from jax.sharding import PartitionSpec as P

f32 = jnp.float32
bf16 = jnp.bfloat16
MESH = pl.DeviceIdType.MESH
HIGHEST = lax.Precision.HIGHEST
NN = ((1,), (0,))
NT = ((1,), (1,))


def dot(a, b, dims):
    return lax.dot_general(a, b, (dims, ((), ())), precision=HIGHEST, preferred_element_type=f32)


def halves(x):
    hi = x.astype(bf16)
    return hi, (x - hi.astype(f32)).astype(bf16)


def dot3(a, b, dims):
    def one(u, v):
        return lax.dot_general(u, v, (dims, ((), ())), preferred_element_type=f32)

    return one(a[0], b[0]) + (one(a[0], b[1]) + one(a[1], b[0]))


def lane_bcast(x, j):
    return jnp.broadcast_to(x[:, j : j + 1], (8, 128))


def sub_bcast(x, k):
    return jnp.broadcast_to(x[k : k + 1, :], (8, 128))


def base64(block, odd, midway):
    lane = lax.broadcasted_iota(jnp.int32, (8, 128), 1)
    sub = lax.broadcasted_iota(jnp.int32, (8, 128), 0)
    to, at = 64 * odd, 64 - 64 * odd
    mine = (lane >= 64) if odd else (lane < 64)
    turned = pltpu.roll(block, 64, 1)
    rows_of = []
    for g in range(8):
        eye = jnp.where(lane == sub + (8 * g + to), 1.0, 0.0).astype(f32)
        rows_of.append(jnp.where(mine, eye, turned[8 * g : 8 * g + 8, :]))
    out = []
    for g in range(8):
        rows = rows_of[g]
        cols = [lane_bcast(rows, at + 8 * g + k) for k in range(8)]
        done = jnp.zeros((8, 128), f32)
        for k in range(8):
            is_k = sub == k
            row = sub_bcast(rows, k)
            pivot = sub_bcast(cols[k], k)
            inv = 1.0 / pivot
            done = jnp.where(is_k, row * lax.rsqrt(pivot), done)
            m = cols[k] * inv
            rows = jnp.where(is_k, row * inv, rows - m * row)
            for j in range(k + 1, 8):
                top = sub_bcast(cols[j], k)
                cols[j] = jnp.where(is_k, top * inv, cols[j] - m * top)
        out.append(jnp.where(mine, done, 0.0))
        if g == 3:
            midway()
        if g < 7:
            tops = [sub_bcast(rows, k) for k in range(8)]
            for i in range(g + 1, 8):
                t = [lane_bcast(rows_of[i], at + 8 * g + k) * tops[k] for k in range(8)]
                rows_of[i] = rows_of[i] - (((t[0] + t[1]) + (t[2] + t[3])) + ((t[4] + t[5]) + (t[6] + t[7])))
    return jnp.concatenate(out, axis=0)


def invert(aw, between):
    following = base64(aw[0:64, 0:128], 0, lambda: between(0))
    between(1)
    for k in range(8):
        odd = k % 2
        w0, r0 = 64 * (k - odd), 64 * k
        own = following
        c0 = 64 * (k + 1) if odd else 64 * k
        c1 = 512 + 64 * (k + 1) if odd else 512 + 64 * (k + 2)
        if k < 7:
            odd_next = (k + 1) % 2
            n0 = 64 * (k + 1 - odd_next)
            left = dot(aw[r0 + 64 : r0 + 128, w0 : w0 + 128], own, NT)
            right = dot(own, aw[w0 : w0 + 128, n0 : n0 + 128], NN)
            block = aw[r0 + 64 : r0 + 128, n0 : n0 + 128] - dot(left, right, NN)
            following = base64(block, odd_next, lambda: between(2 * k + 2))
        right = dot(own, aw[w0 : w0 + 128, c0:c1], NN)
        if k < 7:
            left = dot(aw[r0 + 64 : 512, w0 : w0 + 128], own, NT)
            aw[r0 + 64 : 512, c0:c1] = aw[r0 + 64 : 512, c0:c1] - dot(left, right, NN)
        aw[r0 : r0 + 64, 512:c1] = right[:, 512 - c0 :]
        if k < 7:
            between(2 * k + 3)


class Copies:
    def __init__(self, send, recv):
        self.send, self.recv, self.sent = send, recv, []

    def describe(self, n, src, dst, dev):
        return pltpu.make_async_remote_copy(
            src_ref=src, dst_ref=dst, send_sem=self.send.at[n], recv_sem=self.recv.at[n], device_id=dev, device_id_type=MESH
        )

    def start(self, n, src, dst, dev):
        copy = self.describe(n, src, dst, dev)
        copy.start()
        self.sent.append(copy)

    def arrived(self, n, dst, dev):
        self.describe(n, dst, dst, dev).wait_recv()

    def finish(self):
        for copy in self.sent:
            copy.wait_send()


def kernel(
    b_diag, a_diag, b_panel, a_panel, a_trail,
    diag_out, l_out, n_out, trail_out,
    aw, bd, ad, pr, pc, st, adn, mid, trail, zh, zl,
    send, recv, local, tin, tout,
):
    zlo, x, zhi, y, core = (lax.axis_index(a) for a in ("z_lo", "x", "z_hi", "y", "core"))
    grid_row = zlo * 4 + x
    other = 1 - core

    def up(i, d):
        return lax.rem(i + d, 4)

    load_trail = pltpu.make_async_copy(a_trail, trail, tin.at[0])

    def place(zh_, y_, c_):
        return pl.ds(pl.multiple_of((zh_ * 8 + y_ * 2 + c_) * 32, 32), 32)

    own = place(zhi, y, core)
    own_b = pltpu.make_async_copy(b_panel, pr.at[own, pl.ds(0, 512)], local.at[0])
    own_a = pltpu.make_async_copy(a_panel, pr.at[own, pl.ds(512, 512)], local.at[1])
    half = pl.ds(pl.multiple_of(core * 16, 16), 16)
    own_bd = pltpu.make_async_copy(b_diag.at[half], bd.at[zlo, x, core], local.at[2])
    own_ad = pltpu.make_async_copy(a_diag.at[half], ad.at[zlo, x, core], local.at[3])
    own_bd.start()
    own_b.start()
    own_a.start()
    own_ad.start()

    peers = []
    peers += [{"z_lo": up(zlo, d)} for d in (1, 2, 3)]
    peers += [{"x": up(x, d), "core": c} for d in (1, 3) for c in (0, 1)]
    peers += [{"z_hi": up(zhi, d)} for d in (1, 3)]
    peers += [{"y": up(y, d)} for d in (1, 3)]
    peers += [{"core": other}]
    turned = {"z_lo": zhi, "x": y, "z_hi": zlo, "y": x}
    stays = jnp.logical_and(zlo == zhi, x == y)
    barrier = pltpu.get_barrier_semaphore()
    for dev in peers:
        pl.semaphore_signal(barrier, inc=1, device_id=dev, device_id_type=MESH)

    @pl.when(jnp.logical_not(stays))
    def _():
        pl.semaphore_signal(barrier, inc=1, device_id=turned, device_id_type=MESH)

    pl.semaphore_wait(barrier, len(peers) + 1 - stays.astype(jnp.int32))

    copies = Copies(send, recv)
    X = {1: {"x": up(x, 1)}, -1: {"x": up(x, 3)}}
    Y = {1: {"y": up(y, 1)}, -1: {"y": up(y, 3)}}
    Z = {1: {"z_hi": up(zhi, 1)}, -1: {"z_hi": up(zhi, 3)}}
    CORE = {"core": other}

    def diag_z(base, buf):
        for d in (1, 2, 3):
            copies.start(base + d - 1, buf.at[zlo, x, core], buf.at[zlo, x, core], {"z_lo": up(zlo, d)})

    def diag_x(base, buf):
        for d in (1, 2, 3):
            copies.arrived(base + d - 1, buf.at[up(zlo, 4 - d), x, core], {"z_lo": up(zlo, d)})
        mine = buf.at[:, x, core]
        copies.start(base + 3, mine, mine, X[1])
        copies.start(base + 4, mine, mine, X[-1])
        copies.start(base + 5, mine, mine, CORE)

    def diag_forward(base, buf):
        left, right = up(x, 3), up(x, 1)
        copies.arrived(base + 3, buf.at[:, left, core], X[1])
        part = buf.at[pl.ds(0, 2), left, core]
        copies.start(base + 6, part, part, X[1])
        copies.start(base + 8, buf.at[:, left, core], buf.at[:, left, core], CORE)
        copies.arrived(base + 4, buf.at[:, right, core], X[-1])
        part = buf.at[pl.ds(2, 2), right, core]
        copies.start(base + 7, part, part, X[-1])
        copies.start(base + 9, buf.at[:, right, core], buf.at[:, right, core], CORE)

    def diag_last(base, buf):
        far = up(x, 2)
        copies.arrived(base + 6, buf.at[pl.ds(0, 2), far, core], X[1])
        copies.arrived(base + 7, buf.at[pl.ds(2, 2), far, core], X[-1])
        copies.start(base + 10, buf.at[:, far, core], buf.at[:, far, core], CORE)

    def diag_end(base, buf):
        for n, place_x in ((5, x), (8, up(x, 3)), (9, up(x, 1)), (10, up(x, 2))):
            copies.arrived(base + n, buf.at[:, place_x, other], CORE)

    BD, AD = 0, 11

    ROWZ, ROWY, ROWC = 22, 26, 38
    offsets = (0, 3, 1, 2)

    def piece(o, dy, c):
        return pr.at[place(up(zhi, offsets[o]), up(y, dy), c)]

    def part_of(o, dy, c, h):
        start = (up(zhi, offsets[o]) * 8 + up(y, dy) * 2 + c) * 32 + 16 * h
        return pr.at[pl.ds(pl.multiple_of(start, 16), 16)]

    def rows_z():
        copies.start(ROWZ, piece(0, 0, core), piece(0, 0, core), Z[1])
        copies.start(ROWZ + 1, piece(0, 0, core), piece(0, 0, core), Z[-1])

    def rows_z_forward():
        copies.arrived(ROWZ, piece(1, 0, core), Z[1])
        copies.start(ROWZ + 2, part_of(1, 0, core, 0), part_of(1, 0, core, 0), Z[1])
        copies.arrived(ROWZ + 1, piece(2, 0, core), Z[-1])
        copies.start(ROWZ + 3, part_of(2, 0, core, 1), part_of(2, 0, core, 1), Z[-1])

    def rows_z_last():
        copies.arrived(ROWZ + 2, part_of(3, 0, core, 0), Z[1])
        copies.arrived(ROWZ + 3, part_of(3, 0, core, 1), Z[-1])

    def rows_y(o):
        p = piece(o, 0, core)
        copies.start(ROWY + 3 * o, p, p, Y[1])
        copies.start(ROWY + 3 * o + 1, p, p, Y[-1])
        copies.start(ROWC + 4 * o, p, p, CORE)

    def rows_y_forward(o):
        copies.arrived(ROWY + 3 * o, piece(o, 3, core), Y[1])
        if o < 2:
            copies.start(ROWY + 3 * o + 2, piece(o, 3, core), piece(o, 3, core), Y[1])
        copies.arrived(ROWY + 3 * o + 1, piece(o, 1, core), Y[-1])
        if o >= 2:
            copies.start(ROWY + 3 * o + 2, piece(o, 1, core), piece(o, 1, core), Y[-1])
        copies.start(ROWC + 4 * o + 1, piece(o, 3, core), piece(o, 3, core), CORE)
        copies.start(ROWC + 4 * o + 2, piece(o, 1, core), piece(o, 1, core), CORE)

    def rows_y_last(o):
        copies.arrived(ROWY + 3 * o + 2, piece(o, 2, core), Y[1] if o < 2 else Y[-1])
        copies.start(ROWC + 4 * o + 3, piece(o, 2, core), piece(o, 2, core), CORE)

    def rows_end(o):
        for n, dy in ((0, 0), (1, 3), (2, 1), (3, 2)):
            copies.arrived(ROWC + 4 * o + n, piece(o, dy, other), CORE)

    TURN, COLZ, COLX = 54, 55, 58

    def turn():
        @pl.when(stays)
        def _():
            pltpu.make_async_copy(pr.at[own], st.at[zhi], recv.at[TURN]).start()

        @pl.when(jnp.logical_not(stays))
        def _():
            copies.describe(TURN, pr.at[own], st.at[zhi], turned).start()

    def turned_here():
        @pl.when(stays)
        def _():
            pltpu.make_async_copy(pr.at[own], st.at[zhi], recv.at[TURN]).wait()

        @pl.when(jnp.logical_not(stays))
        def _():
            copies.arrived(TURN, st.at[zlo], turned)

    def turn_sent():
        @pl.when(jnp.logical_not(stays))
        def _():
            copies.describe(TURN, pr.at[own], st.at[zhi], turned).wait_send()

    def cols_z():
        for d in (1, 2, 3):
            copies.start(COLZ + d - 1, st.at[zlo], st.at[zlo], {"z_lo": up(zlo, d)})

    def spot(i, v, s):
        return pc.at[pl.ds(pl.multiple_of((i * 8 + v * 2 + s) * 32, 32), 32)]

    def col_copy(way, h, dev):
        return pltpu.make_async_remote_copy(
            src_ref=st.at[h], dst_ref=spot(lax.rem(h, 2), x, core), send_sem=send.at[COLX + 4 * way + h],
            recv_sem=recv.at[COLX + 4 * way + 2 * lax.rem(h, 2) + core], device_id=dev, device_id_type=MESH,
        )

    def stay_copy(h):
        i = lax.rem(h, 2)
        return pltpu.make_async_copy(st.at[h], spot(i, x, core), recv.at[COLX + 8 + 2 * i + core])

    def cols_x(d):
        h = up(zlo, 4 - d)
        to = lax.div(h, 2)
        if d:
            copies.arrived(COLZ + d - 1, st.at[h], {"z_lo": up(zlo, d)})
        for way, dx in ((0, 1), (1, 3)):
            col_copy(way, h, {"x": up(x, dx), "core": to}).start()

        @pl.when(core == to)
        def _():
            stay_copy(h).start()

        @pl.when(core != to)
        def _():
            col_copy(2, h, CORE).start()

    def cols_x_sent():
        for d in range(4):
            h = up(zlo, 4 - d)
            to = lax.div(h, 2)
            for way, dx in ((0, 1), (1, 3)):
                col_copy(way, h, {"x": up(x, dx), "core": to}).wait_send()

            @pl.when(core != to)
            def _():
                col_copy(2, h, CORE).wait_send()

    FAR = COLX + 16

    def cols_forward(i):
        p = spot(i, up(x, 3), 0)
        copies.arrived(COLX + 2 * i, p, X[1])
        copies.start(FAR + 2 * i, p, p, X[1])
        p = spot(i, up(x, 1), 1)
        copies.arrived(COLX + 4 + 2 * i + 1, p, X[-1])
        copies.start(FAR + 2 * i + 1, p, p, X[-1])

    def cols_end():
        for i in (0, 1):
            copies.arrived(COLX + 2 * i + 1, spot(i, up(x, 3), 1), X[1])
            copies.arrived(COLX + 4 + 2 * i, spot(i, up(x, 1), 0), X[-1])
            for s in (0, 1):
                copies.arrived(COLX + 8 + 2 * i + s, spot(i, x, s), CORE)
                copies.arrived(FAR + 2 * i + s, spot(i, up(x, 2), s), X[1])

    own_bd.wait()
    diag_z(BD, bd)
    own_b.wait()
    own_a.wait()
    turn()
    rows_y(0)
    load_trail.start()
    eye = lax.broadcasted_iota(jnp.int32, (512, 512), 0) == lax.broadcasted_iota(jnp.int32, (512, 512), 1)
    aw[:, 512:] = jnp.where(eye, 1.0, 0.0).astype(f32)
    diag_x(BD, bd)
    diag_forward(BD, bd)
    turned_here()
    cols_z()
    cols_x(0)
    diag_last(BD, bd)
    rows_z()
    own_ad.wait()
    diag_z(AD, ad)
    diag_end(BD, bd)
    aw[:, :512] = bd[...].reshape(512, 512)

    def between(n):
        if n == 0:
            rows_y_forward(0)
        if n == 2:
            rows_y_last(0)
        if n == 5:
            cols_x(1)
        if n == 6:
            cols_x(3)
        if n == 7:
            cols_x(2)
        if n == 8:
            diag_x(AD, ad)
        if n == 9:
            rows_z_forward()
            rows_y(1)
            rows_y(2)
        if n == 11:
            diag_forward(AD, ad)
        if n == 13:
            diag_last(AD, ad)
            rows_z_last()
            rows_y(3)
        if n == 14:
            rows_y_forward(1)
            rows_y_forward(2)
        if n == 15:
            cols_forward(0)
            cols_forward(1)

    invert(aw, between)
    diag_end(AD, ad)
    mid[...] = dot(ad[...].reshape(512, 512), aw[:, 512:], NT)
    w = halves(aw[:, 512:])
    rows_y_last(1)
    rows_y_last(2)
    adn[...] = dot(aw[:, 512:], mid[...], NN)
    diag_out[...] = adn[pl.ds(pl.multiple_of(grid_row * 32, 32), 32), :]
    q = halves(adn[...])
    rows_y_forward(3)
    own_l = dot3(halves(pr[own, 0:512]), w, NT)
    l_out[...] = own_l
    n_out[...] = dot3(halves(pr[own, 512:1024]), w, NT) - dot3(halves(own_l), q, NN)
    rows_y_last(3)
    cols_end()
    col_l = dot3(halves(pc[:, 0:512]), w, NT)
    lh = halves(col_l)
    col_n = dot3(halves(pc[:, 512:1024]), w, NT) - dot3(lh, q, NN)
    col_y = dot3(lh, w, NN)
    col_z = dot3(halves(col_n), w, NN)
    zh[:, 0:512], zl[:, 0:512] = halves(col_z)
    zh[:, 512:1024], zl[:, 512:1024] = halves(col_y)
    load_trail.wait()

    def store(o):
        tile = pl.ds(pl.multiple_of(up(zhi, offsets[o]) * 256, 256), 256)
        return pltpu.make_async_copy(trail.at[tile], trail_out.at[tile], tout.at[o])

    def update(o):
        @pl.loop(0, 2)
        def _(t):
            tile = pl.ds(pl.multiple_of(up(zhi, offsets[o]) * 256 + t * 128, 128), 128)
            trail[tile, :] = trail[tile, :] - dot3(halves(pr[tile, :]), (zh[...], zl[...]), NT)

        store(o).start()

    for o in range(4):
        rows_end(o)
        update(o)

    copies.finish()
    turn_sent()
    cols_x_sent()
    for o in range(4):
        store(o).wait()


def place_results(*refs):
    ins, outs, (few, many, sems_in, sems_out) = refs[:4], refs[4:8], refs[8:]
    ways = [(ins[i], few.at[i], outs[i]) for i in range(3)]
    for t in range(4):
        rows = pl.ds(256 * t, 256)
        ways.append((ins[3].at[rows], many.at[rows], outs[3].at[rows]))
    first = [pltpu.make_async_copy(w[0], w[1], sems_in.at[i]) for i, w in enumerate(ways)]
    then = [pltpu.make_async_copy(w[1], w[2], sems_out.at[i]) for i, w in enumerate(ways)]
    for copy in first:
        copy.start()
    for i, copy in enumerate(then):
        first[i].wait()
        copy.start()
    for copy in then:
        copy.wait()


def shards(*arrays):
    vmem = pl.BlockSpec(memory_space=pltpu.VMEM)
    anywhere = pl.BlockSpec(memory_space=pl.ANY)
    own = jax.ShapeDtypeStruct((32, 512), f32)
    results = pl.pallas_call(
        kernel,
        out_shape=(own, own, own, jax.ShapeDtypeStruct((1024, 512), f32)),
        in_specs=[anywhere] * 5,
        out_specs=(vmem, vmem, vmem, anywhere),
        scratch_shapes=[
            pltpu.VMEM((512, 1024), f32),
            pltpu.VMEM((4, 4, 2, 16, 512), f32),
            pltpu.VMEM((4, 4, 2, 16, 512), f32),
            pltpu.VMEM((1024, 1024), f32),
            pltpu.VMEM((512, 1024), f32),
            pltpu.VMEM((4, 32, 1024), f32),
            pltpu.VMEM((512, 512), f32),
            pltpu.VMEM((512, 512), f32),
            pltpu.VMEM((1024, 512), f32),
            pltpu.VMEM((512, 1024), bf16),
            pltpu.VMEM((512, 1024), bf16),
            pltpu.SemaphoreType.DMA((80,)),
            pltpu.SemaphoreType.DMA((80,)),
            pltpu.SemaphoreType.DMA((4,)),
            pltpu.SemaphoreType.DMA((1,)),
            pltpu.SemaphoreType.DMA((4,)),
        ],
        compiler_params=pltpu.CompilerParams(collective_id=0, has_side_effects=True, vmem_limit_bytes=56 << 20),
        cost_estimate=pl.CostEstimate(flops=10**10, bytes_accessed=8 << 20, transcendentals=0),
    )(*arrays)
    return pl.pallas_call(
        place_results,
        out_shape=(own, own, own, jax.ShapeDtypeStruct((1024, 512), f32)),
        in_specs=[anywhere] * 4,
        out_specs=(anywhere,) * 4,
        scratch_shapes=[
            pltpu.VMEM((3, 32, 512), f32),
            pltpu.VMEM((1024, 512), f32),
            pltpu.SemaphoreType.DMA((7,)),
            pltpu.SemaphoreType.DMA((7,)),
        ],
    )(*results)


def solution(mesh):
    names = ("z_lo", "x", "z_hi", "y", "core")
    split = Mesh(mesh.devices.reshape(4, 4, 4, 4, 2), names)
    row, col = names[:2], names[2:]
    return jax.shard_map(
        shards,
        mesh=split,
        in_specs=(P(row, None), P(row, None), P(names, None), P(names, None), P(row, col)),
        out_specs=(P(row, None), P(names, None), P(names, None), P(row, col)),
        check_vma=False,
    )
```

```python
import functools

import jax
import jax.numpy as jnp
from jax import lax
from jax.experimental import pallas as pl
from jax.experimental.pallas import tpu as pltpu
from jax.sharding import Mesh
from jax.sharding import PartitionSpec as P

f32 = jnp.float32
bf16 = jnp.bfloat16
MESH = pl.DeviceIdType.MESH
HIGHEST = lax.Precision.HIGHEST
NN = ((1,), (0,))
NT = ((1,), (1,))


def dot(a, b, dims):
    return lax.dot_general(a, b, (dims, ((), ())), precision=HIGHEST, preferred_element_type=f32)


def halves(x):
    hi = x.astype(bf16)
    return hi, (x - hi.astype(f32)).astype(bf16)


def dot3(a, b, dims):
    def one(u, v):
        return lax.dot_general(u, v, (dims, ((), ())), preferred_element_type=f32)

    return one(a[0], b[0]) + (one(a[0], b[1]) + one(a[1], b[0]))


def times_turned(a, w):
    near = dot3([v[:, 0:256] for v in a], [v[0:256, 0:256] for v in w], NT)
    return jnp.concatenate([near, dot3(a, [v[256:512] for v in w], NT)], axis=1)


def times(a, w):
    far = dot3([v[:, 256:512] for v in a], [v[256:512, 256:512] for v in w], NN)
    return jnp.concatenate([dot3(a, [v[:, 0:256] for v in w], NN), far], axis=1)


def lane_bcast(x, j):
    return jnp.broadcast_to(x[:, j : j + 1], (8, 128))


def sub_bcast(x, k):
    return jnp.broadcast_to(x[k : k + 1, :], (8, 128))


def base64(block, odd, midway):
    lane = lax.broadcasted_iota(jnp.int32, (8, 128), 1)
    sub = lax.broadcasted_iota(jnp.int32, (8, 128), 0)
    to, at = 64 * odd, 64 - 64 * odd
    mine = (lane >= 64) if odd else (lane < 64)
    turned = pltpu.roll(block, 64, 1)
    rows_of = []
    for g in range(8):
        eye = jnp.where(lane == sub + (8 * g + to), 1.0, 0.0).astype(f32)
        rows_of.append(jnp.where(mine, eye, turned[8 * g : 8 * g + 8, :]))
    out = []
    for g in range(8):
        rows = rows_of[g]
        cols = [lane_bcast(rows, at + 8 * g + k) for k in range(8)]
        done = jnp.zeros((8, 128), f32)
        for k in range(8):
            is_k = sub == k
            row = sub_bcast(rows, k)
            pivot = sub_bcast(cols[k], k)
            inv = 1.0 / pivot
            done = jnp.where(is_k, row * lax.rsqrt(pivot), done)
            m = cols[k] * inv
            rows = jnp.where(is_k, row * inv, rows - m * row)
            for j in range(k + 1, 8):
                top = sub_bcast(cols[j], k)
                cols[j] = jnp.where(is_k, top * inv, cols[j] - m * top)
        out.append(jnp.where(mine, done, 0.0))
        if g == 3:
            midway()
        if g < 7:
            tops = [sub_bcast(rows, k) for k in range(8)]
            for i in range(g + 1, 8):
                t = [lane_bcast(rows_of[i], at + 8 * g + k) * tops[k] for k in range(8)]
                rows_of[i] = rows_of[i] - (((t[0] + t[1]) + (t[2] + t[3])) + ((t[4] + t[5]) + (t[6] + t[7])))
    return jnp.concatenate(out, axis=0)


def invert(aw, between):
    following = base64(aw[0:64, 0:128], 0, lambda: between(0))
    between(1)
    for k in range(8):
        odd = k % 2
        w0, r0 = 64 * (k - odd), 64 * k
        own = following
        c0 = 64 * (k + 1) if odd else 64 * k
        c1 = 512 + 64 * (k + 1) if odd else 512 + 64 * (k + 2)
        if k < 7:
            odd_next = (k + 1) % 2
            n0 = 64 * (k + 1 - odd_next)
            left = dot(aw[r0 + 64 : r0 + 128, w0 : w0 + 128], own, NT)
            right = dot(own, aw[w0 : w0 + 128, n0 : n0 + 128], NN)
            block = aw[r0 + 64 : r0 + 128, n0 : n0 + 128] - dot(left, right, NN)
            following = base64(block, odd_next, lambda: between(2 * k + 2))
        right = dot(own, aw[w0 : w0 + 128, c0:c1], NN)
        if k < 7:
            left = dot(aw[r0 + 64 : 512, w0 : w0 + 128], own, NT)
            aw[r0 + 64 : 512, c0:c1] = aw[r0 + 64 : 512, c0:c1] - dot(left, right, NN)
        aw[r0 : r0 + 64, 512:c1] = right[:, 512 - c0 :]
        if k < 7:
            between(2 * k + 3)


class Copies:
    def __init__(self, send, recv):
        self.send, self.recv, self.sent = send, recv, []

    def describe(self, n, src, dst, dev):
        return pltpu.make_async_remote_copy(
            src_ref=src, dst_ref=dst, send_sem=self.send.at[n], recv_sem=self.recv.at[n], device_id=dev, device_id_type=MESH
        )

    def start(self, n, src, dst, dev):
        copy = self.describe(n, src, dst, dev)
        copy.start()
        self.sent.append(copy)

    def arrived(self, n, dst, dev):
        self.describe(n, dst, dst, dev).wait_recv()

    def finish(self):
        for copy in self.sent:
            copy.wait_send()


def kernel(
    b_diag, a_diag, b_panel, a_panel, a_trail,
    diag_out, l_out, n_out, trail_out,
    aw, bd, ad, pr, pc, st, adn, mid, trail, zh, zl,
    send, recv, local, tin, tout,
):
    zlo, x, zhi, y, core = (lax.axis_index(a) for a in ("z_lo", "x", "z_hi", "y", "core"))
    grid_row = zlo * 4 + x
    other = 1 - core

    def up(i, d):
        return lax.rem(i + d, 4)

    load_trail = pltpu.make_async_copy(a_trail, trail, tin.at[0])

    def place(zh_, y_, c_):
        return pl.ds(pl.multiple_of((zh_ * 8 + y_ * 2 + c_) * 32, 32), 32)

    own = place(zhi, y, core)
    own_b = pltpu.make_async_copy(b_panel, pr.at[own, pl.ds(0, 512)], local.at[0])
    own_a = pltpu.make_async_copy(a_panel, pr.at[own, pl.ds(512, 512)], local.at[1])
    half = pl.ds(pl.multiple_of(core * 16, 16), 16)
    own_bd = pltpu.make_async_copy(b_diag.at[half], bd.at[zlo, x, core], local.at[2])
    own_ad = pltpu.make_async_copy(a_diag.at[half], ad.at[zlo, x, core], local.at[3])
    own_bd.start()
    own_b.start()
    own_a.start()
    own_ad.start()

    peers = []
    peers += [{"z_lo": up(zlo, d)} for d in (1, 2, 3)]
    peers += [{"x": up(x, d), "core": c} for d in (1, 3) for c in (0, 1)]
    peers += [{"z_hi": up(zhi, d)} for d in (1, 3)]
    peers += [{"y": up(y, d)} for d in (1, 3)]
    peers += [{"core": other}]
    turned = {"z_lo": zhi, "x": y, "z_hi": zlo, "y": x}
    stays = jnp.logical_and(zlo == zhi, x == y)
    barrier = pltpu.get_barrier_semaphore()
    for dev in peers:
        pl.semaphore_signal(barrier, inc=1, device_id=dev, device_id_type=MESH)

    @pl.when(jnp.logical_not(stays))
    def _():
        pl.semaphore_signal(barrier, inc=1, device_id=turned, device_id_type=MESH)

    pl.semaphore_wait(barrier, len(peers) + 1 - stays.astype(jnp.int32))

    copies = Copies(send, recv)
    X = {1: {"x": up(x, 1)}, -1: {"x": up(x, 3)}}
    Y = {1: {"y": up(y, 1)}, -1: {"y": up(y, 3)}}
    Z = {1: {"z_hi": up(zhi, 1)}, -1: {"z_hi": up(zhi, 3)}}
    CORE = {"core": other}

    def diag_z(base, buf):
        for d in (1, 2, 3):
            copies.start(base + d - 1, buf.at[zlo, x, core], buf.at[zlo, x, core], {"z_lo": up(zlo, d)})

    def diag_x(base, buf):
        for d in (1, 2, 3):
            copies.arrived(base + d - 1, buf.at[up(zlo, 4 - d), x, core], {"z_lo": up(zlo, d)})
        mine = buf.at[:, x, core]
        copies.start(base + 3, mine, mine, X[1])
        copies.start(base + 4, mine, mine, X[-1])
        copies.start(base + 5, mine, mine, CORE)

    def diag_forward(base, buf):
        left, right = up(x, 3), up(x, 1)
        copies.arrived(base + 3, buf.at[:, left, core], X[1])
        part = buf.at[pl.ds(0, 2), left, core]
        copies.start(base + 6, part, part, X[1])
        copies.start(base + 8, buf.at[:, left, core], buf.at[:, left, core], CORE)
        copies.arrived(base + 4, buf.at[:, right, core], X[-1])
        part = buf.at[pl.ds(2, 2), right, core]
        copies.start(base + 7, part, part, X[-1])
        copies.start(base + 9, buf.at[:, right, core], buf.at[:, right, core], CORE)

    def diag_last(base, buf):
        far = up(x, 2)
        copies.arrived(base + 6, buf.at[pl.ds(0, 2), far, core], X[1])
        copies.arrived(base + 7, buf.at[pl.ds(2, 2), far, core], X[-1])
        copies.start(base + 10, buf.at[:, far, core], buf.at[:, far, core], CORE)

    def diag_end(base, buf):
        for n, place_x in ((5, x), (8, up(x, 3)), (9, up(x, 1)), (10, up(x, 2))):
            copies.arrived(base + n, buf.at[:, place_x, other], CORE)

    BD, AD = 0, 11

    ROWZ, ROWY, ROWC = 22, 26, 38
    offsets = (0, 3, 1, 2)

    def piece(o, dy, c):
        return pr.at[place(up(zhi, offsets[o]), up(y, dy), c)]

    def part_of(o, dy, c, h):
        start = (up(zhi, offsets[o]) * 8 + up(y, dy) * 2 + c) * 32 + 16 * h
        return pr.at[pl.ds(pl.multiple_of(start, 16), 16)]

    def rows_z():
        copies.start(ROWZ, piece(0, 0, core), piece(0, 0, core), Z[1])
        copies.start(ROWZ + 1, piece(0, 0, core), piece(0, 0, core), Z[-1])

    def rows_z_forward():
        copies.arrived(ROWZ, piece(1, 0, core), Z[1])
        copies.start(ROWZ + 2, part_of(1, 0, core, 0), part_of(1, 0, core, 0), Z[1])
        copies.arrived(ROWZ + 1, piece(2, 0, core), Z[-1])
        copies.start(ROWZ + 3, part_of(2, 0, core, 1), part_of(2, 0, core, 1), Z[-1])

    def rows_z_last():
        copies.arrived(ROWZ + 2, part_of(3, 0, core, 0), Z[1])
        copies.arrived(ROWZ + 3, part_of(3, 0, core, 1), Z[-1])

    def rows_y(o):
        p = piece(o, 0, core)
        copies.start(ROWY + 3 * o, p, p, Y[1])
        copies.start(ROWY + 3 * o + 1, p, p, Y[-1])
        copies.start(ROWC + 4 * o, p, p, CORE)

    def rows_y_forward(o):
        copies.arrived(ROWY + 3 * o, piece(o, 3, core), Y[1])
        if o < 2:
            copies.start(ROWY + 3 * o + 2, piece(o, 3, core), piece(o, 3, core), Y[1])
        copies.arrived(ROWY + 3 * o + 1, piece(o, 1, core), Y[-1])
        if o >= 2:
            copies.start(ROWY + 3 * o + 2, piece(o, 1, core), piece(o, 1, core), Y[-1])
        copies.start(ROWC + 4 * o + 1, piece(o, 3, core), piece(o, 3, core), CORE)
        copies.start(ROWC + 4 * o + 2, piece(o, 1, core), piece(o, 1, core), CORE)

    def rows_y_last(o):
        copies.arrived(ROWY + 3 * o + 2, piece(o, 2, core), Y[1] if o < 2 else Y[-1])
        copies.start(ROWC + 4 * o + 3, piece(o, 2, core), piece(o, 2, core), CORE)

    def rows_end(o):
        for n, dy in ((0, 0), (1, 3), (2, 1), (3, 2)):
            copies.arrived(ROWC + 4 * o + n, piece(o, dy, other), CORE)

    TURN, COLZ, COLX = 54, 55, 58

    def turn():
        @pl.when(stays)
        def _():
            pltpu.make_async_copy(pr.at[own], st.at[zhi], recv.at[TURN]).start()

        @pl.when(jnp.logical_not(stays))
        def _():
            copies.describe(TURN, pr.at[own], st.at[zhi], turned).start()

    def turned_here():
        @pl.when(stays)
        def _():
            pltpu.make_async_copy(pr.at[own], st.at[zhi], recv.at[TURN]).wait()

        @pl.when(jnp.logical_not(stays))
        def _():
            copies.arrived(TURN, st.at[zlo], turned)

    def turn_sent():
        @pl.when(jnp.logical_not(stays))
        def _():
            copies.describe(TURN, pr.at[own], st.at[zhi], turned).wait_send()

    def cols_z():
        for d in (1, 2, 3):
            copies.start(COLZ + d - 1, st.at[zlo], st.at[zlo], {"z_lo": up(zlo, d)})

    def spot(i, v, s):
        return pc.at[pl.ds(pl.multiple_of((i * 8 + v * 2 + s) * 32, 32), 32)]

    def col_copy(way, h, dev):
        return pltpu.make_async_remote_copy(
            src_ref=st.at[h], dst_ref=spot(lax.rem(h, 2), x, core), send_sem=send.at[COLX + 4 * way + h],
            recv_sem=recv.at[COLX + 4 * way + 2 * lax.rem(h, 2) + core], device_id=dev, device_id_type=MESH,
        )

    def stay_copy(h):
        i = lax.rem(h, 2)
        return pltpu.make_async_copy(st.at[h], spot(i, x, core), recv.at[COLX + 8 + 2 * i + core])

    def cols_x(d):
        h = up(zlo, 4 - d)
        to = lax.div(h, 2)
        if d:
            copies.arrived(COLZ + d - 1, st.at[h], {"z_lo": up(zlo, d)})
        for way, dx in ((0, 1), (1, 3)):
            col_copy(way, h, {"x": up(x, dx), "core": to}).start()

        @pl.when(core == to)
        def _():
            stay_copy(h).start()

        @pl.when(core != to)
        def _():
            col_copy(2, h, CORE).start()

    def cols_x_sent():
        for d in range(4):
            h = up(zlo, 4 - d)
            to = lax.div(h, 2)
            for way, dx in ((0, 1), (1, 3)):
                col_copy(way, h, {"x": up(x, dx), "core": to}).wait_send()

            @pl.when(core != to)
            def _():
                col_copy(2, h, CORE).wait_send()

    FAR = COLX + 16

    def cols_forward(i):
        p = spot(i, up(x, 3), 0)
        copies.arrived(COLX + 2 * i, p, X[1])
        copies.start(FAR + 2 * i, p, p, X[1])
        p = spot(i, up(x, 1), 1)
        copies.arrived(COLX + 4 + 2 * i + 1, p, X[-1])
        copies.start(FAR + 2 * i + 1, p, p, X[-1])

    def cols_end():
        for i in (0, 1):
            copies.arrived(COLX + 2 * i + 1, spot(i, up(x, 3), 1), X[1])
            copies.arrived(COLX + 4 + 2 * i, spot(i, up(x, 1), 0), X[-1])
            for s in (0, 1):
                copies.arrived(COLX + 8 + 2 * i + s, spot(i, x, s), CORE)
                copies.arrived(FAR + 2 * i + s, spot(i, up(x, 2), s), X[1])

    own_bd.wait()
    diag_z(BD, bd)
    own_b.wait()
    own_a.wait()
    turn()
    rows_y(0)
    load_trail.start()
    eye = lax.broadcasted_iota(jnp.int32, (512, 512), 0) == lax.broadcasted_iota(jnp.int32, (512, 512), 1)
    aw[:, 512:] = jnp.where(eye, 1.0, 0.0).astype(f32)
    diag_x(BD, bd)
    diag_forward(BD, bd)
    turned_here()
    cols_z()
    cols_x(0)
    diag_last(BD, bd)
    rows_z()
    own_ad.wait()
    diag_z(AD, ad)
    diag_end(BD, bd)
    aw[:, :512] = bd[...].reshape(512, 512)

    def between(n):
        if n == 0:
            rows_y_forward(0)
        if n == 2:
            rows_y_last(0)
        if n == 5:
            cols_x(1)
        if n == 6:
            cols_x(3)
        if n == 7:
            cols_x(2)
        if n == 8:
            diag_x(AD, ad)
        if n == 9:
            rows_z_forward()
            rows_y(1)
            rows_y(2)
        if n == 11:
            diag_forward(AD, ad)
        if n == 13:
            diag_last(AD, ad)
            rows_z_last()
            rows_y(3)
        if n == 14:
            rows_y_forward(1)
            rows_y_forward(2)
        if n == 15:
            cols_forward(0)
            cols_forward(1)

    invert(aw, between)
    diag_end(AD, ad)
    w = halves(aw[:, 512:])
    mid[...] = times_turned(halves(ad[...].reshape(512, 512)), w)
    rows_y_last(1)
    rows_y_last(2)
    m = halves(mid[...])
    adn[0:256, :] = dot3([v[0:256, 0:256] for v in w], [v[0:256] for v in m], NN)
    adn[256:512, :] = dot3([v[256:512] for v in w], m, NN)
    diag_out[...] = adn[pl.ds(pl.multiple_of(grid_row * 32, 32), 32), :]
    q = halves(adn[...])
    rows_y_forward(3)
    own_l = times_turned(halves(pr[own, 0:512]), w)
    l_out[...] = own_l
    n_out[...] = times_turned(halves(pr[own, 512:1024]), w) - dot3(halves(own_l), q, NN)
    rows_y_last(3)
    cols_end()
    col_l = times_turned(halves(pc[:, 0:512]), w)
    lh = halves(col_l)
    col_n = times_turned(halves(pc[:, 512:1024]), w) - dot3(lh, q, NN)
    col_y = times(lh, w)
    col_z = times(halves(col_n), w)
    zh[:, 0:512], zl[:, 0:512] = halves(col_z)
    zh[:, 512:1024], zl[:, 512:1024] = halves(col_y)
    load_trail.wait()

    def store(o):
        tile = pl.ds(pl.multiple_of(up(zhi, offsets[o]) * 256, 256), 256)
        return pltpu.make_async_copy(trail.at[tile], trail_out.at[tile], tout.at[o])

    def update(o):
        @pl.loop(0, 2)
        def _(t):
            tile = pl.ds(pl.multiple_of(up(zhi, offsets[o]) * 256 + t * 128, 128), 128)
            trail[tile, :] = trail[tile, :] - dot3(halves(pr[tile, :]), (zh[...], zl[...]), NT)

        store(o).start()

    for o in range(4):
        rows_end(o)
        update(o)

    copies.finish()
    turn_sent()
    cols_x_sent()
    for o in range(4):
        store(o).wait()


def place_results(*refs):
    ins, outs, (few, many, sems_in, sems_out) = refs[:4], refs[4:8], refs[8:]
    ways = [(ins[i], few.at[i], outs[i]) for i in range(3)]
    for t in range(4):
        rows = pl.ds(256 * t, 256)
        ways.append((ins[3].at[rows], many.at[rows], outs[3].at[rows]))
    first = [pltpu.make_async_copy(w[0], w[1], sems_in.at[i]) for i, w in enumerate(ways)]
    then = [pltpu.make_async_copy(w[1], w[2], sems_out.at[i]) for i, w in enumerate(ways)]
    for copy in first:
        copy.start()
    for i, copy in enumerate(then):
        first[i].wait()
        copy.start()
    for copy in then:
        copy.wait()


def shards(*arrays):
    vmem = pl.BlockSpec(memory_space=pltpu.VMEM)
    anywhere = pl.BlockSpec(memory_space=pl.ANY)
    own = jax.ShapeDtypeStruct((32, 512), f32)
    results = pl.pallas_call(
        kernel,
        out_shape=(own, own, own, jax.ShapeDtypeStruct((1024, 512), f32)),
        in_specs=[anywhere] * 5,
        out_specs=(vmem, vmem, vmem, anywhere),
        scratch_shapes=[
            pltpu.VMEM((512, 1024), f32),
            pltpu.VMEM((4, 4, 2, 16, 512), f32),
            pltpu.VMEM((4, 4, 2, 16, 512), f32),
            pltpu.VMEM((1024, 1024), f32),
            pltpu.VMEM((512, 1024), f32),
            pltpu.VMEM((4, 32, 1024), f32),
            pltpu.VMEM((512, 512), f32),
            pltpu.VMEM((512, 512), f32),
            pltpu.VMEM((1024, 512), f32),
            pltpu.VMEM((512, 1024), bf16),
            pltpu.VMEM((512, 1024), bf16),
            pltpu.SemaphoreType.DMA((80,)),
            pltpu.SemaphoreType.DMA((80,)),
            pltpu.SemaphoreType.DMA((4,)),
            pltpu.SemaphoreType.DMA((1,)),
            pltpu.SemaphoreType.DMA((4,)),
        ],
        compiler_params=pltpu.CompilerParams(collective_id=0, has_side_effects=True, vmem_limit_bytes=56 << 20),
        cost_estimate=pl.CostEstimate(flops=10**10, bytes_accessed=8 << 20, transcendentals=0),
    )(*arrays)
    return pl.pallas_call(
        place_results,
        out_shape=(own, own, own, jax.ShapeDtypeStruct((1024, 512), f32)),
        in_specs=[anywhere] * 4,
        out_specs=(anywhere,) * 4,
        scratch_shapes=[
            pltpu.VMEM((3, 32, 512), f32),
            pltpu.VMEM((1024, 512), f32),
            pltpu.SemaphoreType.DMA((7,)),
            pltpu.SemaphoreType.DMA((7,)),
        ],
    )(*results)


def solution(mesh):
    names = ("z_lo", "x", "z_hi", "y", "core")
    split = Mesh(mesh.devices.reshape(4, 4, 4, 4, 2), names)
    row, col = names[:2], names[2:]
    return jax.shard_map(
        shards,
        mesh=split,
        in_specs=(P(row, None), P(row, None), P(names, None), P(names, None), P(row, col)),
        out_specs=(P(row, None), P(names, None), P(names, None), P(row, col)),
        check_vma=False,
    )
```
